256 devices in a mesh: section: 32 (over z_hi, y, x), tensor: 8 (over z_lo, core).
Axes of the slice: x: 4, y: 4, z: 8 (z_hi: 2, z_lo: 4; z = z_hi * 4 + z_lo), core: 2. Of those that a mesh axis runs over, the one named last changes fastest.
Arguments:
- x_fwd: bfloat16 [32, 256, 4096], P('section', 'tensor'), may hold values from -6 to 6
- grad_in: bfloat16 [32, 256, 4096], P('section', 'tensor'), may hold values from -6 to 6
- stash: bfloat16 [32, 2, 256, 4096], P('section', None, 'tensor'), may hold values from -6 to 6
- norm_gain: float32 [32, 4096], P('section'), may hold values from 0.25 to 1.75
- w_query: bfloat16 [32, 4096, 4096], P('section', None, 'tensor')
- w_keyval: bfloat16 [32, 2, 4096, 1024], P('section', None, None, 'tensor')
- w_out: bfloat16 [32, 4096, 4096], P('section', 'tensor'), may hold values from -0.09375 to 0.09375
- slot_table: int32 [32, 2], P('section'), may hold values from 0 to 1
Outputs:
- fwd_out: bfloat16 [32, 256, 4096], P('section', 'tensor')
- bwd_out: bfloat16 [32, 256, 4096], P('section', 'tensor')
- stash_out: bfloat16 [32, 2, 256, 4096], P('section', None, 'tensor')
The draws below stay inside these ranges and needn't reach their ends.
All inputs are finite; a program needn't handle non-finite values.
Results may differ from the reference program's by a relative error of at most 0.02.
The reference program's roundings to bfloat16 on the way (of `payload`, `normed`, `query`, `rounded`, `mixed`, `grad_mixed` and `grad_query`) count: a program that leaves them out, or rounds other values in their place, can miss the bound.
Values may be sent and summed in bfloat16 or wider, within the bound.
No kernel may reach another device: no remote copies, remote signals or barrier semaphores. Data moves between devices by JAX's collectives and lax.ppermute only.
A program may use at most 128 MiB of HBM per device.

```python
import jax
import jax.numpy as jnp
from jax import lax

D = 4096
HEADS = 32
KV_HEADS = 8
HEAD_DIM = 128
TOK = 256
SLOTS = 2
N_SECTION = 32


def draw_w_query(key, part):
    key = jax.random.fold_in(key, 11)
    width = HEADS * HEAD_DIM
    base = jax.random.normal(key, (N_SECTION, D, width), jnp.float32)
    return (base * D ** (-0.5)).astype(jnp.bfloat16)


def draw_w_keyval(key, part):
    key = jax.random.fold_in(key, 12)
    width = KV_HEADS * HEAD_DIM
    base = jax.random.normal(key, (N_SECTION, 2, D, width), jnp.float32)
    return (base * D ** (-0.5)).astype(jnp.bfloat16)


def touch_ends(result, key, low, largest):
    index_at = [jax.random.randint(jax.random.fold_in(key, axis), (), 0, length) for axis, length in enumerate(result.shape)]
    main_axis = result.shape.index(max(result.shape))
    beside = index_at[:main_axis] + [(index_at[main_axis] + 1) % result.shape[main_axis]] + index_at[main_axis + 1:]
    return result.at[tuple(index_at)].set(low).at[tuple(beside)].set(largest)


def levels(key, shape, shards, smallest, top_value):
    def one(dim, blocks):
        steps = jax.random.uniform(jax.random.fold_in(jax.random.fold_in(key, 6), dim), (blocks,), jnp.float32, smallest / len(shards), top_value / len(shards))
        return jnp.repeat(jnp.exp(steps), shape[dim] // blocks).reshape((-1,) + (1,) * (len(shape) - dim - 1))

    loudness = one(*shards[0])
    for cut in shards[1:]:
        loudness = loudness * one(*cut)
    return loudness


def centred(stream_key, extent, scale, reach, pieces=(), kind=jnp.bfloat16):
    factor_of = levels(stream_key, extent, pieces, -0.22, 0.18) if pieces else 1.0
    array = jax.random.normal(stream_key, extent, jnp.float32) * scale * factor_of
    return jnp.minimum(jnp.maximum(array, -reach), reach).astype(kind)


def setup_inputs(seed: int = 0) -> dict:
    splits = jax.random.split(jax.random.key(seed), 9)
    return {
        "x_fwd": centred(splits[0], (N_SECTION, TOK, D), 1.0, 6.0, ((0, 32), (1, 8))),
        "grad_in": centred(splits[1], (N_SECTION, TOK, D), 1.0, 6.0, ((0, 32), (1, 8))),
        "stash": centred(splits[2], (N_SECTION, SLOTS, TOK, D), 1.0, 6.0, ((0, 32), (2, 8))),
        "norm_gain": jnp.clip(1.0 + 0.15 * jax.random.normal(splits[3], (N_SECTION, D), jnp.float32), 0.25, 1.75),
        "w_query": draw_w_query(jax.random.fold_in(splits[8], 71), 0),
        "w_keyval": draw_w_keyval(jax.random.fold_in(splits[8], 71), 0),
        "w_out": centred(splits[6], (N_SECTION, HEADS * HEAD_DIM, D), (HEADS * HEAD_DIM) ** -0.5, 0.09375, ((0, 32), (1, 8))),
        "slot_table": touch_ends(jax.random.randint(splits[7], (N_SECTION, 2), 0, SLOTS), jax.random.fold_in(splits[7], 1), 0, SLOTS - 1).astype(jnp.int32),
    }


EPS = 1e-05
THETA = 500000.0

def rope_tables(tokens, head_size):
    position = jnp.arange(tokens, dtype=jnp.int32).astype(jnp.float32)
    halfway = head_size // 2
    freq = THETA ** (-2.0 * jnp.arange(halfway, dtype=jnp.float32) / head_size)
    angle = position[:, None] * freq[None, :]
    return (jnp.cos(angle), jnp.sin(angle))

def rotate(values, cosine, sine):
    halfway = values.shape[-1] // 2
    first = values[..., :halfway]
    second = values[..., halfway:]
    cos_rows = cosine[:, None, :]
    sin_rows = sine[:, None, :]
    return jnp.concatenate([first * cos_rows - second * sin_rows, second * cos_rows + first * sin_rows], axis=-1)

def normalize(block, gain):
    wide = block.astype(jnp.float32)
    scale = lax.rsqrt(lax.optimization_barrier(jnp.mean(wide * wide, axis=-1, keepdims=True)) + EPS)
    unit = wide * scale
    return ((unit * gain).astype(jnp.bfloat16), unit, scale)

def shape_heads(query, keys, values, cosine, sine):
    tokens = query.shape[0]
    q_heads = query.shape[1] // HEAD_DIM
    k_heads = keys.shape[1] // HEAD_DIM
    query = rotate(query.reshape(tokens, q_heads, HEAD_DIM), cosine, sine).astype(jnp.bfloat16)
    keys = rotate(keys.reshape(tokens, k_heads, HEAD_DIM), cosine, sine).astype(jnp.bfloat16)
    values = values.reshape(tokens, k_heads, HEAD_DIM).astype(jnp.bfloat16)
    return (query.reshape(tokens, k_heads, q_heads // k_heads, HEAD_DIM), keys, values)

def probabilities(query, keys):
    tokens = query.shape[0]
    scores = jnp.einsum('tkgd,ukd->kgtu', query.astype(jnp.float32), keys.astype(jnp.float32)) * HEAD_DIM ** (-0.5)
    causal = jnp.arange(tokens)[:, None] >= jnp.arange(tokens)[None, :]
    scores = jnp.where(causal, scores, -1e+30)
    highest = lax.optimization_barrier(jnp.max(scores, axis=-1, keepdims=True))
    expo = jnp.exp(scores - highest)
    probs = expo / lax.optimization_barrier(jnp.sum(expo, axis=-1, keepdims=True))
    return (probs, probs.astype(jnp.bfloat16))

def mix_values(rounded, values):
    mixed = jnp.einsum('kgtu,ukd->tkgd', rounded.astype(jnp.float32), values.astype(jnp.float32)).astype(jnp.bfloat16)
    return mixed.reshape(mixed.shape[0], -1)

def attention_back(query, keys, values, probs, rounded, grad_mixed, cosine, sine):
    tokens, k_heads, group, _ = query.shape
    grad_heads = grad_mixed.reshape(tokens, k_heads, group, HEAD_DIM).astype(jnp.float32)
    grad_values = jnp.einsum('kgtu,tkgd->ukd', rounded.astype(jnp.float32), grad_heads)
    grad_probs = jnp.einsum('tkgd,ukd->kgtu', grad_heads, values.astype(jnp.float32))
    centre = lax.optimization_barrier(jnp.sum(probs * grad_probs, axis=-1, keepdims=True))
    grad_scores = (probs * (grad_probs - centre) * HEAD_DIM ** (-0.5)).astype(jnp.bfloat16)
    grad_query = jnp.einsum('kgtu,ukd->tkgd', grad_scores.astype(jnp.float32), keys.astype(jnp.float32))
    grad_keys = jnp.einsum('kgtu,tkgd->ukd', grad_scores.astype(jnp.float32), query.astype(jnp.float32))
    grad_query = rotate(grad_query.reshape(tokens, k_heads * group, HEAD_DIM), cosine, -sine)
    grad_keys = rotate(grad_keys, cosine, -sine)
    return (grad_query.reshape(tokens, -1).astype(jnp.bfloat16), grad_keys.reshape(tokens, -1).astype(jnp.bfloat16), grad_values.reshape(tokens, -1).astype(jnp.bfloat16))

def norm_back(grad_normed, unit, scale, gain, upstream):
    weighted = grad_normed * gain
    inner = lax.optimization_barrier(jnp.mean(weighted * unit, axis=-1, keepdims=True))
    return (upstream.astype(jnp.float32) + scale * (weighted - unit * inner)).astype(jnp.bfloat16)

def project(normed, w_query, w_keyval, cosine, sine):
    query = jnp.dot(normed, w_query, preferred_element_type=jnp.float32)
    keys = jnp.dot(normed, w_keyval[0], preferred_element_type=jnp.float32)
    values = jnp.dot(normed, w_keyval[1], preferred_element_type=jnp.float32)
    return shape_heads(query, keys, values, cosine, sine)

def section_pass(bundle):
    x_in, upstream, checkpoint, gain, w_query, w_keyval, w_out = bundle
    tokens = x_in.shape[0]
    cosine, sine = rope_tables(tokens, HEAD_DIM)
    normed_fwd, _, _ = normalize(x_in, gain)
    query, keys, values = project(normed_fwd, w_query, w_keyval, cosine, sine)
    _, rounded = probabilities(query, keys)
    mixed = mix_values(rounded, values)
    output = (x_in.astype(jnp.float32) + jnp.dot(mixed, w_out, preferred_element_type=jnp.float32)).astype(jnp.bfloat16)
    normed_bwd, unit, scale = normalize(checkpoint, gain)
    query_b, keys_b, values_b = project(normed_bwd, w_query, w_keyval, cosine, sine)
    probs_b, rounded_b = probabilities(query_b, keys_b)
    grad_mixed = jnp.dot(upstream, w_out.T, preferred_element_type=jnp.float32).astype(jnp.bfloat16)
    grad_query, grad_keys, grad_values = attention_back(query_b, keys_b, values_b, probs_b, rounded_b, grad_mixed, cosine, sine)
    grad_normed = jnp.dot(grad_query, w_query.T, preferred_element_type=jnp.float32)
    grad_normed = grad_normed + jnp.dot(grad_keys, w_keyval[0].T, preferred_element_type=jnp.float32)
    grad_normed = grad_normed + jnp.dot(grad_values, w_keyval[1].T, preferred_element_type=jnp.float32)
    return (output, norm_back(grad_normed, unit, scale, gain, upstream))

def reference(x_fwd, grad_in, stash, norm_gain, w_query, w_keyval, w_out, slot_table):
    sections = x_fwd.shape[0]
    section_ids = jnp.arange(sections, dtype=jnp.int32)
    is_early = section_ids < sections // 2
    returned = stash[section_ids, slot_table[:, 0]]
    payload = jnp.where(is_early[:, None, None], x_fwd, returned)
    received = payload[::-1]
    own_block = stash[section_ids, slot_table[:, 1]]
    checkpoint = jnp.where(is_early[:, None, None], received, own_block)
    slot_ids = jnp.arange(stash.shape[1], dtype=jnp.int32)
    replace = jnp.logical_and(slot_ids[None, :] == slot_table[:, 0:1], jnp.logical_not(is_early)[:, None])
    stash_out = jnp.where(replace[:, :, None, None], received[:, None], stash)
    outputs, grads = lax.map(section_pass, (x_fwd, grad_in, checkpoint, norm_gain, w_query, w_keyval, w_out))
    fwd_out = jnp.concatenate([jnp.zeros_like(outputs[:1]), outputs[:-1]], axis=0)
    bwd_out = jnp.concatenate([grads[1:], jnp.zeros_like(grads[:1])], axis=0)
    return (fwd_out, bwd_out, stash_out)
```

```python
import jax
import jax.numpy as jnp
from jax import lax
from jax.experimental import pallas as pl
from jax.experimental.pallas import tpu as pltpu
from jax.sharding import PartitionSpec as P

HEAD_DIM = 128
EPS = 1e-05
THETA = 500000.0
CHUNKS = 4
F32 = jnp.float32
BF16 = jnp.bfloat16


def core_swap(value):
    size = lax.axis_size("tensor")
    return lax.ppermute(value, "tensor", [(i, i ^ 1) for i in range(size)])


def chip_swap(value, mask):
    size = lax.axis_size("tensor")
    return lax.ppermute(value, "tensor", [(i, i ^ (2 * mask)) for i in range(size)])


def shifted(value, steps):
    count = lax.axis_size("section")
    return lax.ppermute(
        value, "section", [(i, i + steps) for i in range(count) if 0 <= i + steps < count]
    )


def after(value, *earlier):
    return lax.optimization_barrier((value, *earlier))[0]


def scatter_parts(own, swapped):
    rows = own.shape[0] // 4
    spans = [slice(j * rows, (j + 1) * rows) for j in range(4)]
    return [own[span] + swapped[span].astype(F32) for span in spans]


def local_positions(rows):
    index = lax.axis_index("tensor")
    blocks = [index ^ (2 * j + k) for k in range(2) for j in range(4)]
    start = jnp.stack(blocks) * rows
    return (start[:, None] + jnp.arange(rows, dtype=jnp.int32)[None, :]).reshape(-1)


def rope_tables(position, head_size):
    halfway = head_size // 2
    freq = THETA ** (-2.0 * jnp.arange(halfway, dtype=F32) / head_size)
    angle = position.astype(F32)[:, None] * freq[None, :]
    return (jnp.cos(angle), jnp.sin(angle))


def normalize(block, gain):
    wide = block.astype(F32)
    scale = lax.rsqrt(jnp.mean(wide * wide, axis=-1, keepdims=True) + EPS)
    unit = wide * scale
    return ((unit * gain).astype(BF16), unit, scale)


def swing(values, cosine, sine):
    return values * cosine + pltpu.roll(values, HEAD_DIM // 2, 1) * sine


def dot(left, right, left_dim=1, right_dim=0):
    return lax.dot_general(left, right, (((left_dim,), (right_dim,)), ((), ())), preferred_element_type=F32)


def copy_pieces(pieces, tokens, sems):
    rows = tokens.shape[0] // len(pieces)
    copies = [
        pltpu.make_async_copy(piece, tokens.at[pl.ds(i * rows, rows)], sems.at[i]) for i, piece in enumerate(pieces)
    ]
    for copy in copies:
        copy.start()
    return copies


def qkv_kernel(*refs):
    pieces = refs[:8]
    wq, wkv, cosine, sine, q_out, k_out, v_out, tokens, weights, acc, sems, wsems = refs[8:]
    depth = wq.shape[1] // CHUNKS
    width = wq.shape[2]
    copies = copy_pieces(pieces, tokens, sems)
    loads = []
    for c in range(CHUNKS):
        span = pl.ds(c * depth, depth)
        loads.append(
            [
                pltpu.make_async_copy(wq.at[0, span], weights.at[span, pl.ds(0, width)], wsems.at[c, 0]),
                pltpu.make_async_copy(wkv.at[0, 0, span], weights.at[span, pl.ds(width, HEAD_DIM)], wsems.at[c, 1]),
                pltpu.make_async_copy(
                    wkv.at[0, 1, span], weights.at[span, pl.ds(width + HEAD_DIM, HEAD_DIM)], wsems.at[c, 2]
                ),
            ]
        )
        for load in loads[-1]:
            load.start()
    for copy in copies:
        copy.wait()
    for c in range(CHUNKS):
        for load in loads[c]:
            load.wait()
        part = dot(tokens[:, c * depth : (c + 1) * depth], weights[c * depth : (c + 1) * depth, :])
        if c == 0:
            acc[...] = part
        else:
            acc[...] += part
    cos = cosine[...]
    sin = sine[...]
    for h in range(width // HEAD_DIM):
        cols = slice(h * HEAD_DIM, (h + 1) * HEAD_DIM)
        q_out[:, cols] = swing(acc[:, cols], cos, sin).astype(BF16)
    k_out[...] = swing(acc[:, width : width + HEAD_DIM], cos, sin).astype(BF16)
    v_out[...] = acc[:, width + HEAD_DIM :].astype(BF16)


def head_probs(query, keys, mask):
    scores = dot(query, keys, 1, 1) * HEAD_DIM ** (-0.5)
    scores = jnp.where(mask > 0.0, scores, -1e30)
    expo = jnp.exp(scores - jnp.max(scores, axis=-1, keepdims=True))
    return expo / jnp.sum(expo, axis=-1, keepdims=True)


def attn_fwd_kernel(q, k, v, mask, wo, own_out, other_out, weights, mixed, sems):
    heads = q.shape[1] // HEAD_DIM
    loads = []
    for h in range(heads):
        span = pl.ds(h * HEAD_DIM, HEAD_DIM)
        loads.append(pltpu.make_async_copy(wo.at[0, span], weights.at[span], sems.at[h]))
        loads[-1].start()
    for h in range(heads):
        cols = slice(h * HEAD_DIM, (h + 1) * HEAD_DIM)
        probs = head_probs(q[:, cols], k[...], mask[...])
        mixed[:, cols] = dot(probs.astype(BF16), v[...]).astype(BF16)
    for load in loads:
        load.wait()
    half = q.shape[0] // 2
    step = weights.shape[1] // CHUNKS
    for c in range(CHUNKS):
        cols = slice(c * step, (c + 1) * step)
        part = dot(mixed[...], weights[:, cols])
        own_out[:, cols] = part[:half]
        other_out[:, cols] = part[half:].astype(BF16)


def grad_mixed_kernel(*refs):
    pieces = refs[:8]
    wo, out, tokens, weights, sems, wsems = refs[8:]
    heads = out.shape[1] // HEAD_DIM
    copies = copy_pieces(pieces, tokens, sems)
    loads = []
    for h in range(heads):
        span = pl.ds(h * HEAD_DIM, HEAD_DIM)
        loads.append(pltpu.make_async_copy(wo.at[0, span], weights.at[span], wsems.at[h]))
        loads[-1].start()
    for copy in copies:
        copy.wait()
    for h in range(0, heads, 2):
        loads[h].wait()
        loads[h + 1].wait()
        cols = slice(h * HEAD_DIM, (h + 2) * HEAD_DIM)
        out[:, cols] = dot(tokens[...], weights[cols, :], 1, 1).astype(BF16)


def attn_bwd_kernel(q, k, v, gm, mask, cosine, sine, gq_out, gk_out, gv_out):
    heads = q.shape[1] // HEAD_DIM
    cos = cosine[...]
    sin = -sine[...]
    keys = k[...]
    values = v[...]
    grad_keys = None
    for h in range(heads):
        cols = slice(h * HEAD_DIM, (h + 1) * HEAD_DIM)
        query = q[:, cols]
        grad = gm[:, cols]
        probs = head_probs(query, keys, mask[...])
        grad_probs = dot(grad, values, 1, 1)
        centre = jnp.sum(probs * grad_probs, axis=-1, keepdims=True)
        grad_scores = (probs * (grad_probs - centre) * HEAD_DIM ** (-0.5)).astype(BF16)
        gq_out[:, cols] = swing(dot(grad_scores, keys), cos, sin).astype(BF16)
        more_keys = dot(grad_scores, query, 0, 0)
        more_values = dot(probs.astype(BF16), grad, 0, 0)
        grad_keys = more_keys if grad_keys is None else grad_keys + more_keys
        grad_values = more_values if h == 0 else grad_values + more_values
    gk_out[...] = swing(grad_keys, cos, sin).astype(BF16)
    gv_out[...] = grad_values.astype(BF16)


def call(kernel, outs, moved, hbm, vmem, scratch, flops):
    return pl.pallas_call(
        kernel,
        out_shape=[jax.ShapeDtypeStruct(shape, dtype) for shape, dtype in outs],
        in_specs=[pl.BlockSpec(memory_space=pl.ANY)] * len(moved) + [pl.BlockSpec(memory_space=pltpu.HBM)] * len(hbm) + [pl.BlockSpec(memory_space=pltpu.VMEM)] * len(vmem),
        out_specs=[pl.BlockSpec(memory_space=pltpu.VMEM)] * len(outs),
        scratch_shapes=scratch,
        compiler_params=pltpu.CompilerParams(vmem_limit_bytes=40 * 1024 * 1024),
        cost_estimate=pl.CostEstimate(flops=flops // 64, bytes_accessed=65536, transcendentals=0),
    )(*moved, *hbm, *vmem)


def qkv(pieces, w_query, w_keyval, cosine, sine):
    tokens = 8 * pieces[0].shape[0]
    depth, width = w_query.shape[1:]
    full = width + 2 * HEAD_DIM
    return call(
        qkv_kernel,
        [((tokens, width), BF16), ((tokens, HEAD_DIM), BF16), ((tokens, HEAD_DIM), BF16)],
        pieces,
        [w_query, w_keyval],
        [cosine, sine],
        [
            pltpu.VMEM((tokens, depth), BF16),
            pltpu.VMEM((depth, full), BF16),
            pltpu.VMEM((tokens, full), F32),
            pltpu.SemaphoreType.DMA((8,)),
            pltpu.SemaphoreType.DMA((CHUNKS, 3)),
        ],
        2 * tokens * depth * full,
    )


def attn_fwd(query, keys, values, mask, w_out):
    tokens, width = query.shape
    model = w_out.shape[2]

    def kernel(wo, q, k, v, m, *rest):
        attn_fwd_kernel(q, k, v, m, wo, *rest)

    return call(
        kernel,
        [((tokens // 2, model), F32), ((tokens // 2, model), BF16)],
        [],
        [w_out],
        [query, keys, values, mask],
        [
            pltpu.VMEM((width, model), BF16),
            pltpu.VMEM((tokens, width), BF16),
            pltpu.SemaphoreType.DMA((width // HEAD_DIM,)),
        ],
        2 * tokens * width * model,
    )


def grad_mixing(pieces, w_out):
    tokens = 8 * pieces[0].shape[0]
    width, model = w_out.shape[1:]
    return call(
        grad_mixed_kernel,
        [((tokens, width), BF16)],
        pieces,
        [w_out],
        [],
        [
            pltpu.VMEM((tokens, model), BF16),
            pltpu.VMEM((width, model), BF16),
            pltpu.SemaphoreType.DMA((8,)),
            pltpu.SemaphoreType.DMA((width // HEAD_DIM,)),
        ],
        2 * tokens * width * model,
    )[0]


def attn_bwd(query, keys, values, grad_mixed, mask, cosine, sine):
    tokens, width = query.shape
    return call(
        attn_bwd_kernel,
        [((tokens, width), BF16), ((tokens, HEAD_DIM), BF16), ((tokens, HEAD_DIM), BF16)],
        [],
        [],
        [query, keys, values, grad_mixed, mask, cosine, sine],
        [],
        16 * tokens * tokens * width,
    )


def norm_back(grad_normed, unit, scale, gain, upstream):
    weighted = grad_normed * gain
    inner = jnp.mean(weighted * unit, axis=-1, keepdims=True)
    return (upstream.astype(F32) + scale * (weighted - unit * inner)).astype(BF16)


def back_project(grads, weight):
    return jnp.einsum("tq,dq->td", grads, weight, preferred_element_type=F32)


def body(x_fwd, grad_in, stash, norm_gain, w_query, w_keyval, w_out, slot_table):
    section_idx = lax.axis_index("section")
    sections = lax.axis_size("section")
    is_early = section_idx < sections // 2
    rows = x_fwd.shape[1]
    gain = norm_gain[0]
    weight_q = w_query[0]
    weight_k = w_keyval[0, 0]
    weight_v = w_keyval[0, 1]
    held = stash[0]

    def start_gather(block, tag):
        with jax.named_scope(tag + "_far"):
            far = chip_swap(block, 2)
        with jax.named_scope(tag + "_near"):
            near = chip_swap(block, 1)
        return block, near, far

    def pass_on(far, tag):
        with jax.named_scope(tag + "_last"):
            return chip_swap(far, 1)

    def swap(value, tag):
        with jax.named_scope(tag + "_swap"):
            return core_swap(value)

    own2, near2, far2 = start_gather(grad_in[0], "g2")
    with jax.named_scope("norm_fwd"):
        normed_fwd, _, _ = normalize(x_fwd[0], gain)
    own1, near1, far1 = start_gather(normed_fwd, "g1")
    with jax.named_scope("payload"):
        returned = lax.dynamic_index_in_dim(held, slot_table[0, 0], 0, keepdims=False)
        payload = jnp.where(is_early, x_fwd[0], returned)
        received = lax.ppermute(
            after(payload, normed_fwd), "section", [(i, sections - 1 - i) for i in range(sections)]
        )
    last1 = pass_on(far1, "g1")
    last2 = pass_on(after(far2, far1), "g2")
    mine1 = [own1, near1, far1, last1]
    mine2 = [own2, near2, far2, last2]

    with jax.named_scope("tables"):
        position = local_positions(rows)
        mask = (position[:, None] >= position[None, :]).astype(F32)
        cosine, sine = rope_tables(position, HEAD_DIM)
        cosine, sine = jnp.concatenate([cosine, cosine], axis=1), jnp.concatenate([-sine, sine], axis=1)

    with jax.named_scope("norm_bwd"):
        received = after(received, near1, near2, last1, last2)
        own_block = lax.dynamic_index_in_dim(held, slot_table[0, 1], 0, keepdims=False)
        checkpoint = jnp.where(is_early, received, own_block)
        normed_bwd, unit, scale = normalize(checkpoint, gain)
    own3, near3, far3 = start_gather(normed_bwd, "g3")

    with jax.named_scope("qkv_fwd"):
        pieces = mine1 + [swap(piece, "g1") for piece in mine1]
        pieces = [after(pieces[0], normed_bwd)] + pieces[1:]
        query, keys, values = qkv(pieces, w_query, w_keyval, cosine, sine)
    with jax.named_scope("attn_fwd"):
        part_own, part_other = attn_fwd(query, keys, values, mask, w_out)
    with jax.named_scope("r1_swap"):
        part_other = after(part_other, near3, far3)
        swapped1 = core_swap(part_other)
    last3 = pass_on(after(far3, part_other), "g3")
    mine3 = [own3, near3, far3, last3]
    with jax.named_scope("grad_mixed"):
        pieces = mine2 + [swap(piece, "g2") for piece in mine2]
        pieces = [after(pieces[0], part_other)] + pieces[1:]
        grad_mixed = grad_mixing(pieces, w_out)
    kept1, near1_sum, far1_sum, pass1 = scatter_parts(part_own, swapped1)
    with jax.named_scope("r1_pass"):
        from_near1 = chip_swap(pass1.astype(BF16), 1)
    from_near1 = after(from_near1, last3)
    with jax.named_scope("r1_far"):
        sum_far1 = chip_swap((far1_sum + from_near1.astype(F32)).astype(BF16), 2)
    with jax.named_scope("r1_near"):
        sum_near1 = chip_swap(after(near1_sum, from_near1).astype(BF16), 1)

    with jax.named_scope("qkv_bwd"):
        pieces = mine3 + [swap(piece, "g3") for piece in mine3]
        pieces = [after(pieces[0], from_near1)] + pieces[1:]
        query_b, keys_b, values_b = qkv(pieces, w_query, w_keyval, cosine, sine)
    with jax.named_scope("attn_bwd"):
        grads = attn_bwd(query_b, keys_b, values_b, grad_mixed, mask, cosine, sine)

    with jax.named_scope("fwd_out"):
        attn_part = kept1 + after(sum_near1, grads[0]).astype(F32) + after(sum_far1, grads[0]).astype(F32)
        output = (x_fwd[0].astype(F32) + attn_part).astype(BF16)
        fwd_out = shifted(output[None], 1)
    grads = lax.optimization_barrier((output, *grads))[1:]

    half = 4 * rows

    def grad_rows(low, high):
        total = back_project(grads[0][low:high], weight_q)
        total = total + back_project(grads[1][low:high], weight_k)
        return total + back_project(grads[2][low:high], weight_v)

    with jax.named_scope("back_other"):
        back_other = grad_rows(half, 2 * half).astype(BF16)
    with jax.named_scope("back_own"):
        back_own = grad_rows(0, half)
    with jax.named_scope("r2_swap"):
        swapped2 = core_swap(back_other)
    kept2, near2_sum, far2_sum, pass2 = scatter_parts(back_own, swapped2)
    with jax.named_scope("r2_pass"):
        from_near2 = chip_swap(pass2.astype(BF16), 1)
    with jax.named_scope("r2_far"):
        sum_far2 = chip_swap((far2_sum + from_near2.astype(F32)).astype(BF16), 2)
    with jax.named_scope("r2_near"):
        sum_near2 = chip_swap(after(near2_sum, from_near2).astype(BF16), 1)

    with jax.named_scope("stash_out"):
        slot_ids = jnp.arange(held.shape[0], dtype=jnp.int32)
        replace = jnp.logical_and(slot_ids == slot_table[0, 0], jnp.logical_not(is_early))
        stash_out = jnp.where(replace[:, None, None], received[None], held)[None]
    with jax.named_scope("bwd_out"):
        grad_normed = kept2 + sum_near2.astype(F32) + sum_far2.astype(F32)
        grad_x = norm_back(grad_normed, unit, scale, gain, grad_in[0])
        bwd_out = shifted(grad_x[None], -1)
    return (fwd_out, bwd_out, stash_out)


def solution(mesh):
    placed = (
        P("section", "tensor", None),
        P("section", "tensor", None),
        P("section", None, "tensor", None),
        P("section", None),
        P("section", None, "tensor"),
        P("section", None, None, "tensor"),
        P("section", "tensor", None),
        P("section", None),
    )
    return jax.shard_map(
        body,
        mesh=mesh,
        in_specs=placed,
        out_specs=(
            P("section", "tensor", None),
            P("section", "tensor", None),
            P("section", None, "tensor", None),
        ),
        check_vma=False,
    )
```

```python
import jax
import jax.numpy as jnp
from jax import lax
from jax.experimental import pallas as pl
from jax.experimental.pallas import tpu as pltpu
from jax.sharding import PartitionSpec as P

HEAD_DIM = 128
EPS = 1e-05
THETA = 500000.0
CHUNKS = 4
PIECES = 4
ORDER = (0, 2, 1, 3)
F32 = jnp.float32
BF16 = jnp.bfloat16


def core_swap(value):
    size = lax.axis_size("tensor")
    return lax.ppermute(value, "tensor", [(i, i ^ 1) for i in range(size)])


def chip_swap(value, mask):
    size = lax.axis_size("tensor")
    return lax.ppermute(value, "tensor", [(i, i ^ (2 * mask)) for i in range(size)])


def shifted(value, steps):
    count = lax.axis_size("section")
    return lax.ppermute(
        value, "section", [(i, i + steps) for i in range(count) if 0 <= i + steps < count]
    )


def after(value, *earlier):
    return lax.optimization_barrier((value, *earlier))[0]


def scatter_parts(own, swapped):
    rows = own.shape[0] // 4
    spans = [slice(j * rows, (j + 1) * rows) for j in range(4)]
    return [own[span] + swapped[span].astype(F32) for span in spans]


def local_positions(rows):
    index = lax.axis_index("tensor")
    blocks = [index ^ (2 * j + k) for k in range(2) for j in ORDER]
    start = jnp.stack(blocks) * rows
    return (start[:, None] + jnp.arange(rows, dtype=jnp.int32)[None, :]).reshape(-1)


def rope_tables(position, head_size):
    halfway = head_size // 2
    freq = THETA ** (-2.0 * jnp.arange(halfway, dtype=F32) / head_size)
    angle = position.astype(F32)[:, None] * freq[None, :]
    return (jnp.cos(angle), jnp.sin(angle))


def swing(values, cosine, sine):
    return values * cosine + pltpu.roll(values, HEAD_DIM // 2, 1) * sine


def dot(left, right, left_dim=1, right_dim=0):
    return lax.dot_general(left, right, (((left_dim,), (right_dim,)), ((), ())), preferred_element_type=F32)


def copy_pieces(pieces, tokens, sems):
    copies = []
    low = 0
    for i, piece in enumerate(pieces):
        rows = piece.shape[0]
        copies.append(pltpu.make_async_copy(piece, tokens.at[pl.ds(low, rows)], sems.at[i]))
        copies[-1].start()
        low += rows
    return copies


def qkv_kernel(*refs):
    pieces = refs[:PIECES]
    wq, wkv, cosine, sine, q_out, k_out, v_out, tokens, weights, acc, sems, wsems = refs[PIECES:]
    depth = wq.shape[1] // CHUNKS
    width = wq.shape[2]
    copies = copy_pieces(pieces, tokens, sems)
    loads = []
    for c in range(CHUNKS):
        span = pl.ds(c * depth, depth)
        loads.append(
            [
                pltpu.make_async_copy(wq.at[0, span], weights.at[span, pl.ds(0, width)], wsems.at[c, 0]),
                pltpu.make_async_copy(wkv.at[0, 0, span], weights.at[span, pl.ds(width, HEAD_DIM)], wsems.at[c, 1]),
                pltpu.make_async_copy(
                    wkv.at[0, 1, span], weights.at[span, pl.ds(width + HEAD_DIM, HEAD_DIM)], wsems.at[c, 2]
                ),
            ]
        )
        for load in loads[-1]:
            load.start()
    for copy in copies:
        copy.wait()
    for c in range(CHUNKS):
        for load in loads[c]:
            load.wait()
        part = dot(tokens[:, c * depth : (c + 1) * depth], weights[c * depth : (c + 1) * depth, :])
        if c == 0:
            acc[...] = part
        else:
            acc[...] += part
    cos = cosine[...]
    sin = sine[...]
    for h in range(width // HEAD_DIM):
        cols = slice(h * HEAD_DIM, (h + 1) * HEAD_DIM)
        q_out[:, cols] = swing(acc[:, cols], cos, sin).astype(BF16)
    k_out[...] = swing(acc[:, width : width + HEAD_DIM], cos, sin).astype(BF16)
    v_out[...] = acc[:, width + HEAD_DIM :].astype(BF16)


def head_probs(query, keys, mask):
    scores = dot(query, keys, 1, 1) * HEAD_DIM ** (-0.5)
    scores = jnp.where(mask > 0.0, scores, -1e30)
    expo = jnp.exp(scores - jnp.max(scores, axis=-1, keepdims=True))
    return expo / jnp.sum(expo, axis=-1, keepdims=True)


def attn_fwd_kernel(q, k, v, mask, wo, own_out, other_out, weights, mixed, sems):
    heads = q.shape[1] // HEAD_DIM
    loads = []
    for h in range(heads):
        span = pl.ds(h * HEAD_DIM, HEAD_DIM)
        loads.append(pltpu.make_async_copy(wo.at[0, span], weights.at[span], sems.at[h]))
        loads[-1].start()
    for h in range(heads):
        cols = slice(h * HEAD_DIM, (h + 1) * HEAD_DIM)
        probs = head_probs(q[:, cols], k[...], mask[...])
        mixed[:, cols] = dot(probs.astype(BF16), v[...]).astype(BF16)
    for load in loads:
        load.wait()
    half = q.shape[0] // 2
    step = weights.shape[1] // CHUNKS
    for c in range(CHUNKS):
        cols = slice(c * step, (c + 1) * step)
        part = dot(mixed[...], weights[:, cols])
        own_out[:, cols] = part[:half]
        other_out[:, cols] = part[half:].astype(BF16)


def grad_mixed_kernel(*refs):
    pieces = refs[:PIECES]
    wo, out, tokens, weights, sems, wsems = refs[PIECES:]
    heads = out.shape[1] // HEAD_DIM
    copies = copy_pieces(pieces, tokens, sems)
    loads = []
    for h in range(heads):
        span = pl.ds(h * HEAD_DIM, HEAD_DIM)
        loads.append(pltpu.make_async_copy(wo.at[0, span], weights.at[span], wsems.at[h]))
        loads[-1].start()
    for copy in copies:
        copy.wait()
    for h in range(0, heads, 2):
        loads[h].wait()
        loads[h + 1].wait()
        cols = slice(h * HEAD_DIM, (h + 2) * HEAD_DIM)
        out[:, cols] = dot(tokens[...], weights[cols, :], 1, 1).astype(BF16)


def attn_bwd_kernel(q, k, v, gm, mask, cosine, sine, gq_out, gk_out, gv_out):
    heads = q.shape[1] // HEAD_DIM
    cos = cosine[...]
    sin = -sine[...]
    keys = k[...]
    values = v[...]
    grad_keys = None
    for h in range(heads):
        cols = slice(h * HEAD_DIM, (h + 1) * HEAD_DIM)
        query = q[:, cols]
        grad = gm[:, cols]
        probs = head_probs(query, keys, mask[...])
        grad_probs = dot(grad, values, 1, 1)
        centre = jnp.sum(probs * grad_probs, axis=-1, keepdims=True)
        grad_scores = (probs * (grad_probs - centre) * HEAD_DIM ** (-0.5)).astype(BF16)
        gq_out[:, cols] = swing(dot(grad_scores, keys), cos, sin).astype(BF16)
        more_keys = dot(grad_scores, query, 0, 0)
        more_values = dot(probs.astype(BF16), grad, 0, 0)
        grad_keys = more_keys if grad_keys is None else grad_keys + more_keys
        grad_values = more_values if h == 0 else grad_values + more_values
    gk_out[...] = swing(grad_keys, cos, sin).astype(BF16)
    gv_out[...] = grad_values.astype(BF16)


def call(kernel, outs, moved, hbm, vmem, scratch, flops):
    return pl.pallas_call(
        kernel,
        out_shape=[jax.ShapeDtypeStruct(shape, dtype) for shape, dtype in outs],
        in_specs=[pl.BlockSpec(memory_space=pl.ANY)] * len(moved) + [pl.BlockSpec(memory_space=pl.ANY)] * len(hbm) + [pl.BlockSpec(memory_space=pltpu.VMEM)] * len(vmem),
        out_specs=[pl.BlockSpec(memory_space=pltpu.VMEM)] * len(outs),
        scratch_shapes=scratch,
        compiler_params=pltpu.CompilerParams(vmem_limit_bytes=12 * 1024 * 1024),
        cost_estimate=pl.CostEstimate(flops=flops // 64, bytes_accessed=65536, transcendentals=0),
    )(*moved, *hbm, *vmem)


def qkv(pieces, w_query, w_keyval, cosine, sine):
    tokens = sum(piece.shape[0] for piece in pieces)
    depth, width = w_query.shape[1:]
    full = width + 2 * HEAD_DIM
    return call(
        qkv_kernel,
        [((tokens, width), BF16), ((tokens, HEAD_DIM), BF16), ((tokens, HEAD_DIM), BF16)],
        pieces,
        [w_query, w_keyval],
        [cosine, sine],
        [
            pltpu.VMEM((tokens, depth), BF16),
            pltpu.VMEM((depth, full), BF16),
            pltpu.VMEM((tokens, full), F32),
            pltpu.SemaphoreType.DMA((PIECES,)),
            pltpu.SemaphoreType.DMA((CHUNKS, 3)),
        ],
        2 * tokens * depth * full,
    )


def attn_fwd(query, keys, values, mask, w_out):
    tokens, width = query.shape
    model = w_out.shape[2]

    def kernel(wo, q, k, v, m, *rest):
        attn_fwd_kernel(q, k, v, m, wo, *rest)

    return call(
        kernel,
        [((tokens // 2, model), F32), ((tokens // 2, model), BF16)],
        [],
        [w_out],
        [query, keys, values, mask],
        [
            pltpu.VMEM((width, model), BF16),
            pltpu.VMEM((tokens, width), BF16),
            pltpu.SemaphoreType.DMA((width // HEAD_DIM,)),
        ],
        2 * tokens * width * model,
    )


def grad_mixing(pieces, w_out):
    tokens = sum(piece.shape[0] for piece in pieces)
    width, model = w_out.shape[1:]
    return call(
        grad_mixed_kernel,
        [((tokens, width), BF16)],
        pieces,
        [w_out],
        [],
        [
            pltpu.VMEM((tokens, model), BF16),
            pltpu.VMEM((width, model), BF16),
            pltpu.SemaphoreType.DMA((PIECES,)),
            pltpu.SemaphoreType.DMA((width // HEAD_DIM,)),
        ],
        2 * tokens * width * model,
    )[0]


def attn_bwd(query, keys, values, grad_mixed, mask, cosine, sine):
    tokens, width = query.shape
    return call(
        attn_bwd_kernel,
        [((tokens, width), BF16), ((tokens, HEAD_DIM), BF16), ((tokens, HEAD_DIM), BF16)],
        [],
        [],
        [query, keys, values, grad_mixed, mask, cosine, sine],
        [],
        16 * tokens * tokens * width,
    )


def chosen(slots, column, early, held):
    block = held[0, 0]
    for i in range(1, held.shape[1]):
        block = jnp.where(slots[0, column] == i, held[0, i], block)
    is_early = lax.axis_index("section") < lax.axis_size("section") // 2
    return jnp.where(is_early, early, block)


def payload_kernel(slots, x, held, out):
    out[...] = chosen(slots, 0, x[0], held)


def checkpoint_kernel(slots, received, held, gain, block_out, normed_out):
    block = chosen(slots, 1, received[...], held)
    block_out[...] = block
    normed_out[...] = (unit_rows(block)[0] * gain[...]).astype(BF16)


def with_slots(kernel, outs, slots, *operands):
    return pl.pallas_call(
        kernel,
        out_shape=[jax.ShapeDtypeStruct(shape, BF16) for shape in outs],
        in_specs=[pl.BlockSpec(memory_space=pltpu.SMEM)] + [pl.BlockSpec(memory_space=pltpu.VMEM)] * len(operands),
        out_specs=[pl.BlockSpec(memory_space=pltpu.VMEM)] * len(outs),
    )(slots, *operands)


def unit_rows(block):
    wide = block.astype(F32)
    scale = lax.rsqrt(jnp.mean(wide * wide, axis=-1, keepdims=True) + EPS)
    return wide * scale, scale


def norm_kernel(block, gain, out):
    out[...] = (unit_rows(block[...])[0] * gain[...]).astype(BF16)


def normalize(block, gain):
    return call(norm_kernel, [(block.shape, BF16)], [], [], [block, gain], [], 1)[0]


def norm_back_kernel(kept, near, far, block, gain, upstream, out):
    unit, scale = unit_rows(block[...])
    grad_normed = kept[...] + near[...].astype(F32) + far[...].astype(F32)
    weighted = grad_normed * gain[...]
    inner = jnp.mean(weighted * unit, axis=-1, keepdims=True)
    out[...] = (upstream[0].astype(F32) + scale * (weighted - unit * inner)).astype(BF16)


def norm_back(kept, near, far, block, gain, upstream):
    return call(
        norm_back_kernel, [(block.shape, BF16)], [], [], [kept, near, far, block, gain, upstream], [], 1
    )[0]


def back_project(grads, weight):
    return jnp.einsum("tq,dq->td", grads, weight, preferred_element_type=F32)


def body(x_fwd, grad_in, stash, norm_gain, w_query, w_keyval, w_out, slot_table):
    section_idx = lax.axis_index("section")
    sections = lax.axis_size("section")
    is_early = section_idx < sections // 2
    rows = x_fwd.shape[1]
    weight_q = w_query[0]
    weight_k = w_keyval[0, 0]
    weight_v = w_keyval[0, 1]

    def send(value, mask, tag):
        with jax.named_scope(tag):
            return chip_swap(value, mask)

    def swap(value, tag):
        with jax.named_scope(tag):
            return core_swap(value)

    with jax.named_scope("payload"):
        payload = with_slots(payload_kernel, [x_fwd.shape[1:]], slot_table, x_fwd, stash)[0]
        received = lax.ppermute(payload, "section", [(i, sections - 1 - i) for i in range(sections)])
    with jax.named_scope("norm_fwd"):
        own1 = normalize(after(x_fwd[0], payload), norm_gain)
    far1 = send(own1, 2, "g1_far")
    near1 = send(own1, 1, "g1_near")
    last1 = send(far1, 1, "g1_last")
    own2 = grad_in[0]
    far2 = send(own2, 2, "g2_far")

    with jax.named_scope("tables"):
        position = local_positions(rows)
        mask = (position[:, None] >= position[None, :]).astype(F32)
        cosine, sine = rope_tables(position, HEAD_DIM)
        cosine, sine = jnp.concatenate([cosine, cosine], axis=1), jnp.concatenate([-sine, sine], axis=1)

    with jax.named_scope("norm_bwd"):
        received, far2 = lax.optimization_barrier((received, far2, near1, last1))[:2]
        checkpoint, own3 = with_slots(
            checkpoint_kernel, [received.shape] * 2, slot_table, received, stash, norm_gain
        )
    far3 = send(own3, 2, "g3_far")
    near3 = send(own3, 1, "g3_near")
    pair2 = jnp.concatenate([own2, far2], axis=0)
    near2 = send(pair2, 1, "g2_near")

    with jax.named_scope("qkv_fwd"):
        mine = jnp.concatenate([own1, far1, near1], axis=0)
        pieces = [mine, last1, swap(mine, "g1_swap"), swap(last1, "g1_swaplast")]
        pieces = [after(pieces[0], own3)] + pieces[1:]
        query, keys, values = qkv(pieces, w_query, w_keyval, cosine, sine)
    with jax.named_scope("attn_fwd"):
        part_own, part_other = attn_fwd(query, keys, values, mask, w_out)
    swapped1 = swap(part_other, "r1_swap")
    far3, near3, near2 = lax.optimization_barrier((far3, near3, near2, part_other))[:3]
    last3 = send(far3, 1, "g3_last")
    kept1, far1_sum, near1_sum, pass1 = scatter_parts(part_own, swapped1)
    pass1 = pass1.astype(BF16)
    from_near1 = send(pass1, 1, "r1_pass")
    with jax.named_scope("grad_mixed"):
        pieces = [after(pair2, pass1), near2, swap(pair2, "g2_swap"), swap(near2, "g2_swapnear")]
        grad_mixed = grad_mixing(pieces, w_out)
    from_near1, last3, grad_mixed = lax.optimization_barrier((from_near1, last3, grad_mixed))
    sum_far1 = send((far1_sum + from_near1.astype(F32)).astype(BF16), 2, "r1_far")
    sum_near1 = send(after(near1_sum, from_near1).astype(BF16), 1, "r1_near")

    with jax.named_scope("qkv_bwd"):
        mine = jnp.concatenate([own3, far3, near3], axis=0)
        pieces = [mine, last3, swap(mine, "g3_swap"), swap(last3, "g3_swaplast")]
        pieces = [after(pieces[0], from_near1)] + pieces[1:]
        query_b, keys_b, values_b = qkv(pieces, w_query, w_keyval, cosine, sine)
    with jax.named_scope("attn_bwd"):
        grads = attn_bwd(query_b, keys_b, values_b, grad_mixed, mask, cosine, sine)

    half = 4 * rows

    def grad_rows(low, high):
        total = back_project(grads[0][low:high], weight_q)
        total = total + back_project(grads[1][low:high], weight_k)
        return total + back_project(grads[2][low:high], weight_v)

    with jax.named_scope("back_other"):
        back_other = grad_rows(half, 2 * half).astype(BF16)
    with jax.named_scope("back_own"):
        back_own = grad_rows(0, half)
    swapped2 = swap(back_other, "r2_swap")
    kept2, far2_sum, near2_sum, pass2 = scatter_parts(back_own, swapped2)
    pass2 = pass2.astype(BF16)
    from_near2 = send(pass2, 1, "r2_pass")
    sum_far2 = send((far2_sum + from_near2.astype(F32)).astype(BF16), 2, "r2_far")
    sum_near2 = send(after(near2_sum, from_near2).astype(BF16), 1, "r2_near")

    with jax.named_scope("fwd_out"):
        attn_part = kept1 + after(sum_near1, pass2).astype(F32) + after(sum_far1, pass2).astype(F32)
        output = (x_fwd[0].astype(F32) + attn_part).astype(BF16)
        fwd_out = shifted(output[None], 1)
    with jax.named_scope("stash_out"):
        slot_ids = jnp.arange(stash.shape[1], dtype=jnp.int32)
        replace = jnp.logical_and(slot_ids == slot_table[0, 0], jnp.logical_not(is_early))
        stash_out = jnp.where(replace[:, None, None], received[None], stash[0])[None]
    with jax.named_scope("bwd_out"):
        grad_x = norm_back(kept2, sum_near2, sum_far2, checkpoint, norm_gain, grad_in)
        bwd_out = shifted(grad_x[None], -1)
    return (fwd_out, bwd_out, stash_out)


def solution(mesh):
    placed = (
        P("section", "tensor", None),
        P("section", "tensor", None),
        P("section", None, "tensor", None),
        P("section", None),
        P("section", None, "tensor"),
        P("section", None, None, "tensor"),
        P("section", "tensor", None),
        P("section", None),
    )
    return jax.shard_map(
        body,
        mesh=mesh,
        in_specs=placed,
        out_specs=(
            P("section", "tensor", None),
            P("section", "tensor", None),
            P("section", None, "tensor", None),
        ),
        check_vma=False,
    )
```

```python
import jax
import jax.numpy as jnp
from jax import lax
from jax.experimental import pallas as pl
from jax.experimental.pallas import tpu as pltpu
from jax.sharding import PartitionSpec as P

HEAD_DIM = 128
EPS = 1e-05
THETA = 500000.0
CHUNKS = 4
PIECES = 4
ORDER = (0, 2, 1, 3)
F32 = jnp.float32
BF16 = jnp.bfloat16


def core_swap(value):
    size = lax.axis_size("tensor")
    return lax.ppermute(value, "tensor", [(i, i ^ 1) for i in range(size)])


def chip_swap(value, mask):
    size = lax.axis_size("tensor")
    return lax.ppermute(value, "tensor", [(i, i ^ (2 * mask)) for i in range(size)])


def shifted(value, steps):
    count = lax.axis_size("section")
    return lax.ppermute(
        value, "section", [(i, i + steps) for i in range(count) if 0 <= i + steps < count]
    )


def after(value, *earlier):
    return lax.optimization_barrier((value, *earlier))[0]


def scatter_parts(own, swapped):
    rows = own.shape[0] // 4
    spans = [slice(j * rows, (j + 1) * rows) for j in range(4)]
    return [own[span] + swapped[span].astype(F32) for span in spans]


def local_positions(rows):
    index = lax.axis_index("tensor")
    blocks = [index ^ (2 * j + k) for k in range(2) for j in ORDER]
    start = jnp.stack(blocks) * rows
    return (start[:, None] + jnp.arange(rows, dtype=jnp.int32)[None, :]).reshape(-1)


def rope_tables(position, head_size):
    halfway = head_size // 2
    freq = THETA ** (-2.0 * jnp.arange(halfway, dtype=F32) / head_size)
    angle = position.astype(F32)[:, None] * freq[None, :]
    return (jnp.cos(angle), jnp.sin(angle))


def swing(values, cosine, sine):
    return values * cosine + pltpu.roll(values, HEAD_DIM // 2, 1) * sine


def dot(left, right, left_dim=1, right_dim=0):
    return lax.dot_general(left, right, (((left_dim,), (right_dim,)), ((), ())), preferred_element_type=F32)


def copy_pieces(pieces, tokens, sems):
    copies = []
    low = 0
    for i, piece in enumerate(pieces):
        rows = piece.shape[0]
        copies.append(pltpu.make_async_copy(piece, tokens.at[pl.ds(low, rows)], sems.at[i]))
        copies[-1].start()
        low += rows
    return copies


def qkv_kernel(*refs):
    pieces = refs[:PIECES]
    wq, wkv, cosine, sine, q_out, k_out, v_out, tokens, weights, acc, sems, wsems = refs[PIECES:]
    depth = wq.shape[1] // CHUNKS
    width = wq.shape[2]
    copies = copy_pieces(pieces, tokens, sems)
    loads = []
    for c in range(CHUNKS):
        span = pl.ds(c * depth, depth)
        loads.append(
            [
                pltpu.make_async_copy(wq.at[0, span], weights.at[span, pl.ds(0, width)], wsems.at[c, 0]),
                pltpu.make_async_copy(wkv.at[0, 0, span], weights.at[span, pl.ds(width, HEAD_DIM)], wsems.at[c, 1]),
                pltpu.make_async_copy(
                    wkv.at[0, 1, span], weights.at[span, pl.ds(width + HEAD_DIM, HEAD_DIM)], wsems.at[c, 2]
                ),
            ]
        )
        for load in loads[-1]:
            load.start()
    for copy in copies:
        copy.wait()
    for c in range(CHUNKS):
        for load in loads[c]:
            load.wait()
        part = dot(tokens[:, c * depth : (c + 1) * depth], weights[c * depth : (c + 1) * depth, :])
        if c == 0:
            acc[...] = part
        else:
            acc[...] += part
    cos = cosine[...]
    sin = sine[...]
    for h in range(width // HEAD_DIM):
        cols = slice(h * HEAD_DIM, (h + 1) * HEAD_DIM)
        q_out[:, cols] = swing(acc[:, cols], cos, sin).astype(BF16)
    k_out[...] = swing(acc[:, width : width + HEAD_DIM], cos, sin).astype(BF16)
    v_out[...] = acc[:, width + HEAD_DIM :].astype(BF16)


def head_probs(query, keys, mask):
    scores = dot(query, keys, 1, 1) * HEAD_DIM ** (-0.5)
    scores = jnp.where(mask > 0.0, scores, -1e30)
    expo = jnp.exp(scores - jnp.max(scores, axis=-1, keepdims=True))
    return expo / jnp.sum(expo, axis=-1, keepdims=True)


def attn_fwd_kernel(q, k, v, mask, wo, own_out, other_out, weights, mixed, sems):
    heads = q.shape[1] // HEAD_DIM
    loads = []
    for h in range(heads):
        span = pl.ds(h * HEAD_DIM, HEAD_DIM)
        loads.append(pltpu.make_async_copy(wo.at[0, span], weights.at[span], sems.at[h]))
        loads[-1].start()
    for h in range(heads):
        cols = slice(h * HEAD_DIM, (h + 1) * HEAD_DIM)
        probs = head_probs(q[:, cols], k[...], mask[...])
        mixed[:, cols] = dot(probs.astype(BF16), v[...]).astype(BF16)
    for load in loads:
        load.wait()
    half = q.shape[0] // 2
    step = weights.shape[1] // CHUNKS
    for c in range(CHUNKS):
        cols = slice(c * step, (c + 1) * step)
        part = dot(mixed[...], weights[:, cols])
        own_out[:, cols] = part[:half]
        other_out[:, cols] = part[half:].astype(BF16)


def grad_mixed_kernel(*refs):
    pieces = refs[:PIECES]
    wo, out, tokens, weights, sems, wsems = refs[PIECES:]
    heads = out.shape[1] // HEAD_DIM
    copies = copy_pieces(pieces, tokens, sems)
    loads = []
    for h in range(heads):
        span = pl.ds(h * HEAD_DIM, HEAD_DIM)
        loads.append(pltpu.make_async_copy(wo.at[0, span], weights.at[span], wsems.at[h]))
        loads[-1].start()
    for copy in copies:
        copy.wait()
    for h in range(0, heads, 2):
        loads[h].wait()
        loads[h + 1].wait()
        cols = slice(h * HEAD_DIM, (h + 2) * HEAD_DIM)
        out[:, cols] = dot(tokens[...], weights[cols, :], 1, 1).astype(BF16)


def attn_bwd_kernel(q, k, v, gm, mask, cosine, sine, gq_out, gk_out, gv_out):
    heads = q.shape[1] // HEAD_DIM
    cos = cosine[...]
    sin = -sine[...]
    keys = k[...]
    values = v[...]
    grad_keys = None
    for h in range(heads):
        cols = slice(h * HEAD_DIM, (h + 1) * HEAD_DIM)
        query = q[:, cols]
        grad = gm[:, cols]
        probs = head_probs(query, keys, mask[...])
        grad_probs = dot(grad, values, 1, 1)
        centre = jnp.sum(probs * grad_probs, axis=-1, keepdims=True)
        grad_scores = (probs * (grad_probs - centre) * HEAD_DIM ** (-0.5)).astype(BF16)
        gq_out[:, cols] = swing(dot(grad_scores, keys), cos, sin).astype(BF16)
        more_keys = dot(grad_scores, query, 0, 0)
        more_values = dot(probs.astype(BF16), grad, 0, 0)
        grad_keys = more_keys if grad_keys is None else grad_keys + more_keys
        grad_values = more_values if h == 0 else grad_values + more_values
    gk_out[...] = swing(grad_keys, cos, sin).astype(BF16)
    gv_out[...] = grad_values.astype(BF16)


def call(kernel, outs, moved, hbm, vmem, scratch, flops):
    return pl.pallas_call(
        kernel,
        out_shape=[jax.ShapeDtypeStruct(shape, dtype) for shape, dtype in outs],
        in_specs=[pl.BlockSpec(memory_space=pl.ANY)] * len(moved) + [pl.BlockSpec(memory_space=pl.ANY)] * len(hbm) + [pl.BlockSpec(memory_space=pltpu.VMEM)] * len(vmem),
        out_specs=[pl.BlockSpec(memory_space=pltpu.VMEM)] * len(outs),
        scratch_shapes=scratch,
        compiler_params=pltpu.CompilerParams(vmem_limit_bytes=12 * 1024 * 1024),
        cost_estimate=pl.CostEstimate(flops=flops // 64, bytes_accessed=65536, transcendentals=0),
    )(*moved, *hbm, *vmem)


def qkv(pieces, w_query, w_keyval, cosine, sine):
    tokens = sum(piece.shape[0] for piece in pieces)
    depth, width = w_query.shape[1:]
    full = width + 2 * HEAD_DIM
    return call(
        qkv_kernel,
        [((tokens, width), BF16), ((tokens, HEAD_DIM), BF16), ((tokens, HEAD_DIM), BF16)],
        pieces,
        [w_query, w_keyval],
        [cosine, sine],
        [
            pltpu.VMEM((tokens, depth), BF16),
            pltpu.VMEM((depth, full), BF16),
            pltpu.VMEM((tokens, full), F32),
            pltpu.SemaphoreType.DMA((PIECES,)),
            pltpu.SemaphoreType.DMA((CHUNKS, 3)),
        ],
        2 * tokens * depth * full,
    )


def attn_fwd(query, keys, values, mask, w_out):
    tokens, width = query.shape
    model = w_out.shape[2]

    def kernel(wo, q, k, v, m, *rest):
        attn_fwd_kernel(q, k, v, m, wo, *rest)

    return call(
        kernel,
        [((tokens // 2, model), F32), ((tokens // 2, model), BF16)],
        [],
        [w_out],
        [query, keys, values, mask],
        [
            pltpu.VMEM((width, model), BF16),
            pltpu.VMEM((tokens, width), BF16),
            pltpu.SemaphoreType.DMA((width // HEAD_DIM,)),
        ],
        2 * tokens * width * model,
    )


def grad_mixing(pieces, w_out):
    tokens = sum(piece.shape[0] for piece in pieces)
    width, model = w_out.shape[1:]
    return call(
        grad_mixed_kernel,
        [((tokens, width), BF16)],
        pieces,
        [w_out],
        [],
        [
            pltpu.VMEM((tokens, model), BF16),
            pltpu.VMEM((width, model), BF16),
            pltpu.SemaphoreType.DMA((PIECES,)),
            pltpu.SemaphoreType.DMA((width // HEAD_DIM,)),
        ],
        2 * tokens * width * model,
    )[0]


def attn_bwd(query, keys, values, grad_mixed, mask, cosine, sine):
    tokens, width = query.shape
    return call(
        attn_bwd_kernel,
        [((tokens, width), BF16), ((tokens, HEAD_DIM), BF16), ((tokens, HEAD_DIM), BF16)],
        [],
        [],
        [query, keys, values, grad_mixed, mask, cosine, sine],
        [],
        16 * tokens * tokens * width,
    )


def chosen(slots, column, early, held):
    block = held[0, 0]
    for i in range(1, held.shape[1]):
        block = jnp.where(slots[0, column] == i, held[0, i], block)
    is_early = lax.axis_index("section") < lax.axis_size("section") // 2
    return jnp.where(is_early, early, block)


def payload_kernel(slots, x, held, out):
    out[...] = chosen(slots, 0, x[0], held)


def checkpoint_kernel(slots, received, held, gain, block_out, normed_out):
    block = chosen(slots, 1, received[...], held)
    block_out[...] = block
    normed_out[...] = (unit_rows(block)[0] * gain[...]).astype(BF16)


def with_slots(kernel, outs, slots, *operands):
    return pl.pallas_call(
        kernel,
        out_shape=[jax.ShapeDtypeStruct(shape, BF16) for shape in outs],
        in_specs=[pl.BlockSpec(memory_space=pltpu.SMEM)] + [pl.BlockSpec(memory_space=pltpu.VMEM)] * len(operands),
        out_specs=[pl.BlockSpec(memory_space=pltpu.VMEM)] * len(outs),
    )(slots, *operands)


def unit_rows(block):
    wide = block.astype(F32)
    scale = lax.rsqrt(jnp.mean(wide * wide, axis=-1, keepdims=True) + EPS)
    return wide * scale, scale


def norm_kernel(block, gain, out):
    out[...] = (unit_rows(block[...])[0] * gain[...]).astype(BF16)


def normalize(block, gain):
    return call(norm_kernel, [(block.shape, BF16)], [], [], [block, gain], [], 1)[0]


def norm_back_kernel(kept, near, far, block, gain, upstream, out):
    unit, scale = unit_rows(block[...])
    grad_normed = kept[...] + near[...].astype(F32) + far[...].astype(F32)
    weighted = grad_normed * gain[...]
    inner = jnp.mean(weighted * unit, axis=-1, keepdims=True)
    out[...] = (upstream[0].astype(F32) + scale * (weighted - unit * inner)).astype(BF16)


def norm_back(kept, near, far, block, gain, upstream):
    return call(
        norm_back_kernel, [(block.shape, BF16)], [], [], [kept, near, far, block, gain, upstream], [], 1
    )[0]


def back_project(grads, weight):
    return jnp.einsum("tq,dq->td", grads, weight, preferred_element_type=F32)


def body(x_fwd, grad_in, stash, norm_gain, w_query, w_keyval, w_out, slot_table):
    section_idx = lax.axis_index("section")
    sections = lax.axis_size("section")
    is_early = section_idx < sections // 2
    rows = x_fwd.shape[1]
    weight_q = w_query[0]
    weight_k = w_keyval[0, 0]
    weight_v = w_keyval[0, 1]

    def send(value, mask, tag):
        with jax.named_scope(tag):
            return chip_swap(value, mask)

    def swap(value, tag):
        with jax.named_scope(tag):
            return core_swap(value)

    with jax.named_scope("payload"):
        payload = with_slots(payload_kernel, [x_fwd.shape[1:]], slot_table, x_fwd, stash)[0]
        received = lax.ppermute(payload, "section", [(i, sections - 1 - i) for i in range(sections)])
    with jax.named_scope("norm_fwd"):
        own1 = normalize(after(x_fwd[0], payload), norm_gain)
    far1 = send(own1, 2, "g1_far")
    near1 = send(own1, 1, "g1_near")
    last1 = send(far1, 1, "g1_last")
    own2 = grad_in[0]
    far2 = send(own2, 2, "g2_far")

    with jax.named_scope("tables"):
        position = local_positions(rows)
        mask = (position[:, None] >= position[None, :]).astype(F32)
        cosine, sine = rope_tables(position, HEAD_DIM)
        cosine, sine = jnp.concatenate([cosine, cosine], axis=1), jnp.concatenate([-sine, sine], axis=1)

    with jax.named_scope("norm_bwd"):
        received, far2 = lax.optimization_barrier((received, far2, near1, last1))[:2]
        checkpoint, own3 = with_slots(
            checkpoint_kernel, [received.shape] * 2, slot_table, received, stash, norm_gain
        )
    far3 = send(own3, 2, "g3_far")
    near3 = send(own3, 1, "g3_near")
    pair2 = jnp.concatenate([own2, far2], axis=0)
    near2 = send(pair2, 1, "g2_near")

    with jax.named_scope("qkv_fwd"):
        mine = jnp.concatenate([own1, far1, near1], axis=0)
        pieces = [mine, last1, swap(mine, "g1_swap"), swap(last1, "g1_swaplast")]
        pieces = [after(pieces[0], own3)] + pieces[1:]
        query, keys, values = qkv(pieces, w_query, w_keyval, cosine, sine)
    with jax.named_scope("attn_fwd"):
        part_own, part_other = attn_fwd(query, keys, values, mask, w_out)
    swapped1 = swap(part_other, "r1_swap")
    far3, near3, near2 = lax.optimization_barrier((far3, near3, near2, part_other))[:3]
    last3 = send(far3, 1, "g3_last")
    kept1, far1_sum, near1_sum, pass1 = scatter_parts(part_own, swapped1)
    pass1 = pass1.astype(BF16)
    from_near1 = send(pass1, 1, "r1_pass")
    with jax.named_scope("grad_mixed"):
        pieces = [after(pair2, pass1), near2, swap(pair2, "g2_swap"), swap(near2, "g2_swapnear")]
        grad_mixed = grad_mixing(pieces, w_out)
    from_near1, last3, grad_mixed = lax.optimization_barrier((from_near1, last3, grad_mixed))
    sum_far1 = send((far1_sum + from_near1.astype(F32)).astype(BF16), 2, "r1_far")
    sum_near1 = send(after(near1_sum, from_near1).astype(BF16), 1, "r1_near")

    with jax.named_scope("qkv_bwd"):
        mine = jnp.concatenate([own3, far3, near3], axis=0)
        pieces = [mine, last3, swap(mine, "g3_swap"), swap(last3, "g3_swaplast")]
        pieces = [after(pieces[0], from_near1)] + pieces[1:]
        query_b, keys_b, values_b = qkv(pieces, w_query, w_keyval, cosine, sine)
    with jax.named_scope("attn_bwd"):
        grads = attn_bwd(query_b, keys_b, values_b, grad_mixed, mask, cosine, sine)

    half = 4 * rows

    def grad_rows(low, high):
        total = back_project(grads[0][low:high], weight_q)
        total = total + back_project(grads[1][low:high], weight_k)
        return total + back_project(grads[2][low:high], weight_v)

    with jax.named_scope("back_other"):
        back_other = grad_rows(half, 2 * half).astype(BF16)
    with jax.named_scope("back_own"):
        back_own = grad_rows(0, half)
    swapped2 = swap(back_other, "r2_swap")
    kept2, far2_sum, near2_sum, pass2 = scatter_parts(back_own, swapped2)
    pass2 = pass2.astype(BF16)
    from_near2 = send(pass2, 1, "r2_pass")
    sum_far2 = send((far2_sum + from_near2.astype(F32)).astype(BF16), 2, "r2_far")
    sum_near2 = send(after(near2_sum, from_near2).astype(BF16), 1, "r2_near")

    with jax.named_scope("fwd_out"):
        attn_part = kept1 + after(sum_near1, pass2).astype(F32) + after(sum_far1, pass2).astype(F32)
        output = (x_fwd[0].astype(F32) + attn_part).astype(BF16)
        middle = sections // 2
        hops = [(i, 0 if i == middle - 1 else i + 1) for i in range(sections - 1)]
        first = lax.ppermute(output[None], "section", hops)
        second = lax.ppermute(first, "section", [(0, middle)])
        kept_first = jnp.where(section_idx == 0, jnp.zeros_like(first), first)
        fwd_out = jnp.where(section_idx == middle, second, kept_first)
    with jax.named_scope("stash_out"):
        slot_ids = jnp.arange(stash.shape[1], dtype=jnp.int32)
        replace = jnp.logical_and(slot_ids == slot_table[0, 0], jnp.logical_not(is_early))
        stash_out = jnp.where(replace[:, None, None], received[None], stash[0])[None]
    with jax.named_scope("bwd_out"):
        grad_x = norm_back(kept2, sum_near2, sum_far2, checkpoint, norm_gain, grad_in)
        bwd_out = shifted(grad_x[None], -1)
    return (fwd_out, bwd_out, stash_out)


def solution(mesh):
    placed = (
        P("section", "tensor", None),
        P("section", "tensor", None),
        P("section", None, "tensor", None),
        P("section", None),
        P("section", None, "tensor"),
        P("section", None, None, "tensor"),
        P("section", "tensor", None),
        P("section", None),
    )
    return jax.shard_map(
        body,
        mesh=mesh,
        in_specs=placed,
        out_specs=(
            P("section", "tensor", None),
            P("section", "tensor", None),
            P("section", None, "tensor", None),
        ),
        check_vma=False,
    )
```

```python
import jax
import jax.numpy as jnp
from jax import lax
from jax.experimental import pallas as pl
from jax.experimental.pallas import tpu as pltpu
from jax.sharding import PartitionSpec as P

HEAD_DIM = 128
EPS = 1e-05
THETA = 500000.0
CHUNKS = 4
PIECES = 4
ORDER = (0, 2, 1, 3)
F32 = jnp.float32
BF16 = jnp.bfloat16


def core_swap(value):
    size = lax.axis_size("tensor")
    return lax.ppermute(value, "tensor", [(i, i ^ 1) for i in range(size)])


def chip_swap(value, mask):
    size = lax.axis_size("tensor")
    return lax.ppermute(value, "tensor", [(i, i ^ (2 * mask)) for i in range(size)])


def shifted(value, steps):
    count = lax.axis_size("section")
    return lax.ppermute(
        value, "section", [(i, i + steps) for i in range(count) if 0 <= i + steps < count]
    )


def after(value, *earlier):
    return lax.optimization_barrier((value, *earlier))[0]


def scatter_parts(own, swapped):
    rows = own.shape[0] // 4
    spans = [slice(j * rows, (j + 1) * rows) for j in range(4)]
    return [own[span] + swapped[span].astype(F32) for span in spans]


def local_positions(rows):
    index = lax.axis_index("tensor")
    blocks = [index ^ (2 * j + k) for k in range(2) for j in ORDER]
    start = jnp.stack(blocks) * rows
    return (start[:, None] + jnp.arange(rows, dtype=jnp.int32)[None, :]).reshape(-1)


def rope_tables(position, head_size):
    halfway = head_size // 2
    freq = THETA ** (-2.0 * jnp.arange(halfway, dtype=F32) / head_size)
    angle = position.astype(F32)[:, None] * freq[None, :]
    return (jnp.cos(angle), jnp.sin(angle))


def swing(values, cosine, sine):
    return values * cosine + pltpu.roll(values, HEAD_DIM // 2, 1) * sine


def dot(left, right, left_dim=1, right_dim=0):
    return lax.dot_general(left, right, (((left_dim,), (right_dim,)), ((), ())), preferred_element_type=F32)


def copy_pieces(pieces, tokens, sems):
    copies = []
    low = 0
    for i, piece in enumerate(pieces):
        rows = piece.shape[0]
        copies.append(pltpu.make_async_copy(piece, tokens.at[pl.ds(low, rows)], sems.at[i]))
        copies[-1].start()
        low += rows
    return copies


def qkv_kernel(*refs):
    pieces = refs[:PIECES]
    wq, wkv, cosine, sine, q_out, k_out, v_out, tokens, weights, acc, sems, wsems = refs[PIECES:]
    depth = wq.shape[1] // CHUNKS
    width = wq.shape[2]
    copies = copy_pieces(pieces, tokens, sems)
    loads = []
    for c in range(CHUNKS):
        span = pl.ds(c * depth, depth)
        loads.append(
            [
                pltpu.make_async_copy(wq.at[0, span], weights.at[span, pl.ds(0, width)], wsems.at[c, 0]),
                pltpu.make_async_copy(wkv.at[0, 0, span], weights.at[span, pl.ds(width, HEAD_DIM)], wsems.at[c, 1]),
                pltpu.make_async_copy(
                    wkv.at[0, 1, span], weights.at[span, pl.ds(width + HEAD_DIM, HEAD_DIM)], wsems.at[c, 2]
                ),
            ]
        )
        for load in loads[-1]:
            load.start()
    for copy in copies:
        copy.wait()
    for c in range(CHUNKS):
        for load in loads[c]:
            load.wait()
        part = dot(tokens[:, c * depth : (c + 1) * depth], weights[c * depth : (c + 1) * depth, :])
        if c == 0:
            acc[...] = part
        else:
            acc[...] += part
    cos = cosine[...]
    sin = sine[...]
    for h in range(width // HEAD_DIM):
        cols = slice(h * HEAD_DIM, (h + 1) * HEAD_DIM)
        q_out[:, cols] = swing(acc[:, cols], cos, sin).astype(BF16)
    k_out[...] = swing(acc[:, width : width + HEAD_DIM], cos, sin).astype(BF16)
    v_out[...] = acc[:, width + HEAD_DIM :].astype(BF16)


def head_probs(query, keys, mask):
    scores = dot(query, keys, 1, 1) * HEAD_DIM ** (-0.5)
    scores = jnp.where(mask > 0.0, scores, -1e30)
    expo = jnp.exp(scores - jnp.max(scores, axis=-1, keepdims=True))
    return expo / jnp.sum(expo, axis=-1, keepdims=True)


def attn_fwd_kernel(q, k, v, mask, wo, own_out, other_out, weights, mixed, sems):
    heads = q.shape[1] // HEAD_DIM
    loads = []
    for h in range(heads):
        span = pl.ds(h * HEAD_DIM, HEAD_DIM)
        loads.append(pltpu.make_async_copy(wo.at[0, span], weights.at[span], sems.at[h]))
        loads[-1].start()
    for h in range(heads):
        cols = slice(h * HEAD_DIM, (h + 1) * HEAD_DIM)
        probs = head_probs(q[:, cols], k[...], mask[...])
        mixed[:, cols] = dot(probs.astype(BF16), v[...]).astype(BF16)
    for load in loads:
        load.wait()
    half = q.shape[0] // 2
    step = weights.shape[1] // CHUNKS
    for c in range(CHUNKS):
        cols = slice(c * step, (c + 1) * step)
        part = dot(mixed[...], weights[:, cols])
        own_out[:, cols] = part[:half]
        other_out[:, cols] = part[half:].astype(BF16)


def grad_mixed_kernel(*refs):
    pieces = refs[:PIECES]
    wo, out, tokens, weights, sems, wsems = refs[PIECES:]
    heads = out.shape[1] // HEAD_DIM
    copies = copy_pieces(pieces, tokens, sems)
    loads = []
    for h in range(heads):
        span = pl.ds(h * HEAD_DIM, HEAD_DIM)
        loads.append(pltpu.make_async_copy(wo.at[0, span], weights.at[span], wsems.at[h]))
        loads[-1].start()
    for copy in copies:
        copy.wait()
    for h in range(0, heads, 2):
        loads[h].wait()
        loads[h + 1].wait()
        cols = slice(h * HEAD_DIM, (h + 2) * HEAD_DIM)
        out[:, cols] = dot(tokens[...], weights[cols, :], 1, 1).astype(BF16)


def attn_bwd_kernel(q, k, v, gm, mask, cosine, sine, gq_out, gk_out, gv_out):
    heads = q.shape[1] // HEAD_DIM
    cos = cosine[...]
    sin = -sine[...]
    keys = k[...]
    values = v[...]
    grad_keys = None
    for h in range(heads):
        cols = slice(h * HEAD_DIM, (h + 1) * HEAD_DIM)
        query = q[:, cols]
        grad = gm[:, cols]
        probs = head_probs(query, keys, mask[...])
        grad_probs = dot(grad, values, 1, 1)
        centre = jnp.sum(probs * grad_probs, axis=-1, keepdims=True)
        grad_scores = (probs * (grad_probs - centre) * HEAD_DIM ** (-0.5)).astype(BF16)
        gq_out[:, cols] = swing(dot(grad_scores, keys), cos, sin).astype(BF16)
        more_keys = dot(grad_scores, query, 0, 0)
        more_values = dot(probs.astype(BF16), grad, 0, 0)
        grad_keys = more_keys if grad_keys is None else grad_keys + more_keys
        grad_values = more_values if h == 0 else grad_values + more_values
    gk_out[...] = swing(grad_keys, cos, sin).astype(BF16)
    gv_out[...] = grad_values.astype(BF16)


def call(kernel, outs, moved, hbm, vmem, scratch, flops):
    return pl.pallas_call(
        kernel,
        out_shape=[jax.ShapeDtypeStruct(shape, dtype) for shape, dtype in outs],
        in_specs=[pl.BlockSpec(memory_space=pl.ANY)] * len(moved) + [pl.BlockSpec(memory_space=pl.ANY)] * len(hbm) + [pl.BlockSpec(memory_space=pltpu.VMEM)] * len(vmem),
        out_specs=[pl.BlockSpec(memory_space=pltpu.VMEM)] * len(outs),
        scratch_shapes=scratch,
        compiler_params=pltpu.CompilerParams(vmem_limit_bytes=12 * 1024 * 1024),
        cost_estimate=pl.CostEstimate(flops=flops // 64, bytes_accessed=65536, transcendentals=0),
    )(*moved, *hbm, *vmem)


def qkv(pieces, w_query, w_keyval, cosine, sine):
    tokens = sum(piece.shape[0] for piece in pieces)
    depth, width = w_query.shape[1:]
    full = width + 2 * HEAD_DIM
    return call(
        qkv_kernel,
        [((tokens, width), BF16), ((tokens, HEAD_DIM), BF16), ((tokens, HEAD_DIM), BF16)],
        pieces,
        [w_query, w_keyval],
        [cosine, sine],
        [
            pltpu.VMEM((tokens, depth), BF16),
            pltpu.VMEM((depth, full), BF16),
            pltpu.VMEM((tokens, full), F32),
            pltpu.SemaphoreType.DMA((PIECES,)),
            pltpu.SemaphoreType.DMA((CHUNKS, 3)),
        ],
        2 * tokens * depth * full,
    )


def attn_fwd(query, keys, values, mask, w_out):
    tokens, width = query.shape
    model = w_out.shape[2]

    def kernel(wo, q, k, v, m, *rest):
        attn_fwd_kernel(q, k, v, m, wo, *rest)

    return call(
        kernel,
        [((tokens // 2, model), F32), ((tokens // 2, model), BF16)],
        [],
        [w_out],
        [query, keys, values, mask],
        [
            pltpu.VMEM((width, model), BF16),
            pltpu.VMEM((tokens, width), BF16),
            pltpu.SemaphoreType.DMA((width // HEAD_DIM,)),
        ],
        2 * tokens * width * model,
    )


def grad_mixing(pieces, w_out):
    tokens = sum(piece.shape[0] for piece in pieces)
    width, model = w_out.shape[1:]
    return call(
        grad_mixed_kernel,
        [((tokens, width), BF16)],
        pieces,
        [w_out],
        [],
        [
            pltpu.VMEM((tokens, model), BF16),
            pltpu.VMEM((width, model), BF16),
            pltpu.SemaphoreType.DMA((PIECES,)),
            pltpu.SemaphoreType.DMA((width // HEAD_DIM,)),
        ],
        2 * tokens * width * model,
    )[0]


def attn_bwd(query, keys, values, grad_mixed, mask, cosine, sine):
    tokens, width = query.shape
    return call(
        attn_bwd_kernel,
        [((tokens, width), BF16), ((tokens, HEAD_DIM), BF16), ((tokens, HEAD_DIM), BF16)],
        [],
        [],
        [query, keys, values, grad_mixed, mask, cosine, sine],
        [],
        16 * tokens * tokens * width,
    )


def chosen(slots, column, early, held):
    block = held[0, 0]
    for i in range(1, held.shape[1]):
        block = jnp.where(slots[0, column] == i, held[0, i], block)
    is_early = lax.axis_index("section") < lax.axis_size("section") // 2
    return jnp.where(is_early, early, block)


def first_kernel(slots, x, held, gain, payload_out, normed_out):
    block = x[0]
    payload_out[...] = chosen(slots, 0, block, held)
    normed_out[...] = (unit_rows(block)[0] * gain[...]).astype(BF16)


def checkpoint_kernel(slots, received, held, gain, block_out, normed_out):
    block = chosen(slots, 1, received[...], held)
    block_out[...] = block
    normed_out[...] = (unit_rows(block)[0] * gain[...]).astype(BF16)


def with_slots(kernel, outs, slots, *operands):
    return pl.pallas_call(
        kernel,
        out_shape=[jax.ShapeDtypeStruct(shape, BF16) for shape in outs],
        in_specs=[pl.BlockSpec(memory_space=pltpu.SMEM)] + [pl.BlockSpec(memory_space=pltpu.VMEM)] * len(operands),
        out_specs=[pl.BlockSpec(memory_space=pltpu.VMEM)] * len(outs),
    )(slots, *operands)


def unit_rows(block):
    wide = block.astype(F32)
    scale = lax.rsqrt(jnp.mean(wide * wide, axis=-1, keepdims=True) + EPS)
    return wide * scale, scale


def norm_back_kernel(kept, near, far, block, gain, upstream, out):
    unit, scale = unit_rows(block[...])
    grad_normed = kept[...] + near[...].astype(F32) + far[...].astype(F32)
    weighted = grad_normed * gain[...]
    inner = jnp.mean(weighted * unit, axis=-1, keepdims=True)
    out[...] = (upstream[0].astype(F32) + scale * (weighted - unit * inner)).astype(BF16)


def norm_back(kept, near, far, block, gain, upstream):
    return call(
        norm_back_kernel, [(block.shape, BF16)], [], [], [kept, near, far, block, gain, upstream], [], 1
    )[0]


def back_project(grads, weight):
    return jnp.einsum("tq,dq->td", grads, weight, preferred_element_type=F32)


def body(x_fwd, grad_in, stash, norm_gain, w_query, w_keyval, w_out, slot_table):
    section_idx = lax.axis_index("section")
    sections = lax.axis_size("section")
    is_early = section_idx < sections // 2
    rows = x_fwd.shape[1]
    weight_q = w_query[0]
    weight_k = w_keyval[0, 0]
    weight_v = w_keyval[0, 1]

    def send(value, mask, tag):
        with jax.named_scope(tag):
            return chip_swap(value, mask)

    def swap(value, tag):
        with jax.named_scope(tag):
            return core_swap(value)

    with jax.named_scope("payload"):
        payload, own1 = with_slots(first_kernel, [x_fwd.shape[1:]] * 2, slot_table, x_fwd, stash, norm_gain)
        received = lax.ppermute(payload, "section", [(i, sections - 1 - i) for i in range(sections)])
    far1 = send(own1, 2, "g1_far")
    near1 = send(own1, 1, "g1_near")
    last1 = send(far1, 1, "g1_last")
    own2 = grad_in[0]
    far2 = send(own2, 2, "g2_far")

    with jax.named_scope("tables"):
        position = local_positions(rows)
        mask = (position[:, None] >= position[None, :]).astype(F32)
        cosine, sine = rope_tables(position, HEAD_DIM)
        cosine, sine = jnp.concatenate([cosine, cosine], axis=1), jnp.concatenate([-sine, sine], axis=1)

    with jax.named_scope("norm_bwd"):
        received, far2 = lax.optimization_barrier((received, far2, near1, last1))[:2]
        checkpoint, own3 = with_slots(
            checkpoint_kernel, [received.shape] * 2, slot_table, received, stash, norm_gain
        )
    far3 = send(own3, 2, "g3_far")
    near3 = send(own3, 1, "g3_near")
    pair2 = jnp.concatenate([own2, far2], axis=0)
    near2 = send(pair2, 1, "g2_near")

    with jax.named_scope("qkv_fwd"):
        mine = jnp.concatenate([own1, far1, near1], axis=0)
        pieces = [mine, last1, swap(mine, "g1_swap"), swap(last1, "g1_swaplast")]
        pieces = [after(pieces[0], own3)] + pieces[1:]
        query, keys, values = qkv(pieces, w_query, w_keyval, cosine, sine)
    with jax.named_scope("attn_fwd"):
        part_own, part_other = attn_fwd(query, keys, values, mask, w_out)
    swapped1 = swap(part_other, "r1_swap")
    far3, near3, near2 = lax.optimization_barrier((far3, near3, near2, part_other))[:3]
    last3 = send(far3, 1, "g3_last")
    kept1, far1_sum, near1_sum, pass1 = scatter_parts(part_own, swapped1)
    pass1 = pass1.astype(BF16)
    from_near1 = send(pass1, 1, "r1_pass")
    with jax.named_scope("grad_mixed"):
        pieces = [after(pair2, pass1), near2, swap(pair2, "g2_swap"), swap(near2, "g2_swapnear")]
        grad_mixed = grad_mixing(pieces, w_out)
    from_near1, last3, grad_mixed = lax.optimization_barrier((from_near1, last3, grad_mixed))
    sum_far1 = send((far1_sum + from_near1.astype(F32)).astype(BF16), 2, "r1_far")
    sum_near1 = send(after(near1_sum, from_near1).astype(BF16), 1, "r1_near")

    with jax.named_scope("qkv_bwd"):
        mine = jnp.concatenate([own3, far3, near3], axis=0)
        pieces = [mine, last3, swap(mine, "g3_swap"), swap(last3, "g3_swaplast")]
        pieces = [after(pieces[0], from_near1)] + pieces[1:]
        query_b, keys_b, values_b = qkv(pieces, w_query, w_keyval, cosine, sine)
    with jax.named_scope("attn_bwd"):
        grads = attn_bwd(query_b, keys_b, values_b, grad_mixed, mask, cosine, sine)

    half = 4 * rows

    def grad_rows(low, high):
        total = back_project(grads[0][low:high], weight_q)
        total = total + back_project(grads[1][low:high], weight_k)
        return total + back_project(grads[2][low:high], weight_v)

    with jax.named_scope("back_other"):
        back_other = grad_rows(half, 2 * half).astype(BF16)
    with jax.named_scope("back_own"):
        back_own = grad_rows(0, half)
    swapped2 = swap(back_other, "r2_swap")
    kept2, far2_sum, near2_sum, pass2 = scatter_parts(back_own, swapped2)
    pass2 = pass2.astype(BF16)
    from_near2 = send(pass2, 1, "r2_pass")
    sum_far2 = send((far2_sum + from_near2.astype(F32)).astype(BF16), 2, "r2_far")
    sum_near2 = send(after(near2_sum, from_near2).astype(BF16), 1, "r2_near")

    with jax.named_scope("fwd_out"):
        attn_part = kept1 + after(sum_near1, pass2).astype(F32) + after(sum_far1, pass2).astype(F32)
        output = (x_fwd[0].astype(F32) + attn_part).astype(BF16)
        middle = sections // 2
        hops = [(i, 0 if i == middle - 1 else i + 1) for i in range(sections - 1)]
        first = lax.ppermute(output[None], "section", hops)
        second = lax.ppermute(first, "section", [(0, middle)])
        kept_first = jnp.where(section_idx == 0, jnp.zeros_like(first), first)
        fwd_out = jnp.where(section_idx == middle, second, kept_first)
    with jax.named_scope("stash_out"):
        slot_ids = jnp.arange(stash.shape[1], dtype=jnp.int32)
        replace = jnp.logical_and(slot_ids == slot_table[0, 0], jnp.logical_not(is_early))
        stash_out = jnp.where(replace[:, None, None], received[None], stash[0])[None]
    with jax.named_scope("bwd_out"):
        grad_x = norm_back(kept2, sum_near2, sum_far2, checkpoint, norm_gain, grad_in)
        bwd_out = shifted(grad_x[None], -1)
    return (fwd_out, bwd_out, stash_out)


def solution(mesh):
    placed = (
        P("section", "tensor", None),
        P("section", "tensor", None),
        P("section", None, "tensor", None),
        P("section", None),
        P("section", None, "tensor"),
        P("section", None, None, "tensor"),
        P("section", "tensor", None),
        P("section", None),
    )
    return jax.shard_map(
        body,
        mesh=mesh,
        in_specs=placed,
        out_specs=(
            P("section", "tensor", None),
            P("section", "tensor", None),
            P("section", None, "tensor", None),
        ),
        check_vma=False,
    )
```
